512 devices in a mesh: blk: 32 (over y, x_lo, core), rep: 16 (over z, x_hi).
Axes of the slice: x: 4 (x_hi: 2, x_lo: 2; x = x_hi * 2 + x_lo), y: 8, z: 8, core: 2. Of those that a mesh axis runs over, the one named last changes fastest.
Arguments:
- visit_embeds: bfloat16 [16, 4096, 1024], P('rep', 'blk'), may hold values from -6 to 6
- result_embeds: bfloat16 [16, 4096, 1024], P('rep', 'blk'), may hold values from -6 to 6
- matched_result_index: int32 [16, 4096], P('rep'), may hold values from 0 to 4095, each once within a row
- logit_stretch: float32 [], replicated, may hold values from 1 to 3
- logit_offset: float32 [], replicated, may hold values from -4 to -1
Outputs:
- d_sessions: float32 [16, 4096, 1024], P('rep', 'blk')
- d_outcomes: float32 [16, 4096, 1024], P('rep', 'blk')
- loss: float32 [], replicated
- d_temperature: float32 [], replicated
- d_bias: float32 [], replicated
The draws below stay inside these ranges and needn't reach their ends.
Inputs may be any that keep to these rules, and one draw needn't show every extreme that they name: `matched_result_index`: each row names every outcome of its batch exactly once.
All inputs are finite; a program needn't handle non-finite values.
Results may differ from the reference program's by a relative error of at most 0.002.
Values may be sent and summed in bfloat16 or wider, within the bound.
No kernel may reach another device: no remote copies, remote signals or barrier semaphores. Data moves between devices by JAX's collectives and lax.ppermute only.
A program may use at most 64 MiB of HBM per device.

```python
import math
import jax
import jax.numpy as jnp
from jax import lax

D = 1024
BATCH = 4096
GROUPS = 16


def block_levels(key, shape, shards, smallest, top_value):
    gain = 1.0
    for dim, parts in shards:
        heights = jax.random.uniform(jax.random.fold_in(jax.random.fold_in(key, 6), dim), (parts,), jnp.float32, smallest / len(shards), top_value / len(shards))
        gain = gain * jnp.repeat(jnp.exp(heights), shape[dim] // parts).reshape((-1,) + (1,) * (len(shape) - 1 - dim))
    return gain


def gaussian(key, dims, spread, most, shards=(), held_as=jnp.bfloat16):
    factor_of = block_levels(key, dims, shards, -0.22, 0.18) if shards else 1.0
    result = jax.random.normal(key, dims, jnp.float32) * spread * factor_of
    return jnp.minimum(jnp.maximum(result, -most), most).astype(held_as)


def setup_inputs(seed: int = 0) -> dict:
    streams_of = jax.random.split(jax.random.key(seed), 6)
    visit_embeds = gaussian(streams_of[0], (GROUPS, BATCH, D), 1.0, 6.0, ((0, 16), (1, 32)))
    result_embeds = gaussian(streams_of[1], (GROUPS, BATCH, D), 1.0, 6.0, ((0, 16), (1, 32)))
    matched_result_index = jax.vmap(lambda own: jax.random.permutation(own, BATCH))(jax.random.split(streams_of[2], GROUPS)).reshape((GROUPS, BATCH)).astype(jnp.int32)
    logit_stretch = jnp.clip(jnp.exp(jax.random.uniform(streams_of[3], (), jnp.float32, math.log(1.0), math.log(3.0))), 1.0, 3.0)
    logit_offset = jnp.clip(jax.random.uniform(streams_of[4], (), jnp.float32, -4.0, -1.0), -4.0, -1.0)
    return {"visit_embeds": visit_embeds, "result_embeds": result_embeds, "matched_result_index": matched_result_index, "logit_stretch": logit_stretch, "logit_offset": logit_offset}


def solitary_group(element_sequence, logit_stretch, logit_offset):
    visit_embeds, result_embeds, matched_result_index = element_sequence
    stretch_multiplier = 1.0 / math.sqrt(D)
    following_entry = jnp.dot(visit_embeds, result_embeds.T, preferred_element_type=jnp.float32) * stretch_multiplier
    initial_entry = logit_stretch * following_entry + logit_offset
    cols = jnp.arange(BATCH, dtype=jnp.int32)
    z_val = jnp.where(matched_result_index[:, None] == cols[None, :], 1.0, -1.0).astype(jnp.float32)
    derivative_entry = -z_val * jax.nn.sigmoid(-z_val * initial_entry)
    multiplier = (derivative_entry * (logit_stretch * stretch_multiplier)).astype(jnp.bfloat16)
    visit_derivative = jnp.dot(multiplier, result_embeds, preferred_element_type=jnp.float32)
    result_derivative = jnp.dot(multiplier.T, visit_embeds, preferred_element_type=jnp.float32)
    objective_accumulated = jnp.sum(jax.nn.softplus(-z_val * initial_entry))
    return (visit_derivative, result_derivative, objective_accumulated, jnp.sum(derivative_entry * following_entry), jnp.sum(derivative_entry))

def reference(visit_embeds, result_embeds, matched_result_index, logit_stretch, logit_offset):
    visit_derivative, result_derivative, objective_accumulated, stretch_accumulated, offset_accumulated = lax.map(lambda element_sequence: solitary_group(element_sequence, logit_stretch, logit_offset), (visit_embeds, result_embeds, matched_result_index))
    number_entries = 1.0 * GROUPS * BATCH * BATCH
    return (visit_derivative, result_derivative, jnp.sum(objective_accumulated) / number_entries, jnp.sum(stretch_accumulated) / number_entries, jnp.sum(offset_accumulated) / number_entries)
```

```python
import functools
import math

import jax
import jax.numpy as jnp
from jax import lax
from jax.experimental import pallas as pl
from jax.experimental.pallas import tpu as pltpu
from jax.sharding import Mesh
from jax.sharding import PartitionSpec as P

NY, NX, NC, NZ, NH = 8, 2, 2, 8, 2
BLK, REP = ("y", "x", "c"), ("z", "h")


def at(y, x, c):
    return (y % NY) * NX * NC + (x % NX) * NC + (c % NC)


def move(dy=0, dx=0, dc=0):
    return [
        (at(y, x, c), at(y + dy, x + dx, c + dc))
        for y in range(NY)
        for x in range(NX)
        for c in range(NC)
    ]


def split(step):
    return [
        (at(y, x, c), at(y + (step if c == 0 else -step), x, c))
        for y in range(NY)
        for x in range(NX)
        for c in range(NC)
    ]


def pair_kernel(unit, first, n, base_ref, to_ref, scal_ref, idx_ref, v_ref, *rest):
    r_refs, rest = rest[:n], rest[n:]
    if not first:
        ds_in, sums_in, _, *rest = rest
    ds_ref, sums_ref, do_ref, held, sems = rest
    stretch = scal_ref[0]
    offset = scal_ref[1]
    scale = stretch * unit
    matched = idx_ref[...]
    m = v_ref.shape[0]
    width = r_refs[0].shape[0]
    v = v_ref[...]
    sums = [jnp.zeros((8, m), jnp.float32) for _ in range(3)]
    copies = []
    for k, r_ref in enumerate(r_refs):
        r = r_ref[...]
        y = (
            lax.dot_general(r, v, (((1,), (1,)), ((), ())), preferred_element_type=jnp.float32)
            * unit
        )
        x = stretch * y + offset
        hit = base_ref[k] + lax.broadcasted_iota(jnp.int32, (width, m), 0) == matched
        t = jnp.where(hit, -x, x)
        e = jnp.exp(-jnp.abs(t))
        inv = 1.0 / (1.0 + e)
        sig = jnp.where(t >= 0, inv, e * inv)
        grad = jnp.where(hit, -sig, sig)
        for i, a in enumerate((jnp.maximum(t, 0.0) + jnp.log1p(e), grad * y, grad)):
            sums[i] += jnp.sum(a.reshape(width // 8, 8, m), axis=0)
        coef = (grad * scale).astype(jnp.bfloat16)
        slot = k % 2
        if k >= 2:
            copies[k - 2].wait()
        held[slot] = jnp.dot(coef, v, preferred_element_type=jnp.float32)
        rows = pl.ds(pl.multiple_of(to_ref[k] * width, width), width)
        copies.append(pltpu.make_async_copy(held.at[slot], do_ref.at[rows], sems.at[slot]))
        copies[k].start()
        part = lax.dot_general(
            coef, r, (((0,), (0,)), ((), ())), preferred_element_type=jnp.float32
        )
        if k:
            ds_ref[...] += part
        elif first:
            ds_ref[...] = part
        else:
            ds_ref[...] = ds_in[...] + part
    for i, a in enumerate(sums):
        s = a[:, :128]
        for j in range(128, m, 128):
            s += a[:, j : j + 128]
        s = jnp.sum(s, axis=0, keepdims=True)
        sums_ref[i : i + 1, :] = s if first else s + sums_in[i : i + 1, :]
    for copy in copies[-2:]:
        copy.wait()


def pairs(base, to, scal, idx, v, rs, carry=()):
    m, d = v.shape
    width = rs[0].shape[0]
    n = len(rs)
    cols = n * width
    vm = pl.BlockSpec(memory_space=pltpu.VMEM)
    sm = pl.BlockSpec(memory_space=pltpu.SMEM)
    hbm = pl.BlockSpec(memory_space=pl.ANY)
    args = [base, to, scal, idx, v, *rs, *carry]
    first = len(args) - 3
    return pl.pallas_call(
        functools.partial(pair_kernel, 1.0 / math.sqrt(d), not carry, n),
        out_shape=[
            jax.ShapeDtypeStruct((m, d), jnp.float32),
            jax.ShapeDtypeStruct((3, 128), jnp.float32),
            jax.ShapeDtypeStruct((NY * width, d), jnp.float32),
        ],
        in_specs=[sm, sm, sm] + [vm] * (2 + n) + ([vm, vm, hbm] if carry else []),
        out_specs=[vm, vm, hbm],
        scratch_shapes=[
            pltpu.VMEM((2, width, d), jnp.float32),
            pltpu.SemaphoreType.DMA((2,)),
        ],
        input_output_aliases={first + i: i for i in range(3)} if carry else {},
        compiler_params=pltpu.CompilerParams(vmem_limit_bytes=48 * 1024 * 1024),
        cost_estimate=pl.CostEstimate(
            flops=6 * m * cols * d,
            bytes_accessed=2 * (m + cols) * d + 4 * (2 * m + cols) * d,
            transcendentals=3 * m * cols,
        ),
    )(*args)


def local(visit_embeds, result_embeds, matched_result_index, logit_stretch, logit_offset):
    v0 = visit_embeds[0]
    r0 = result_embeds[0]
    rows = v0.shape[0]
    index = matched_result_index[0]
    batch = index.shape[0]
    me = lax.axis_index(BLK)
    y, x, c = me // (NX * NC), (me // NC) % NX, me % NC
    tie = lambda *xs: lax.optimization_barrier(xs)
    send = lambda a, p: lax.ppermute(a, BLK, p)
    right, left = move(dy=1), move(dy=-1)

    v = jnp.concatenate([v0, send(v0, move(dc=1))], axis=0)
    l1, u1 = send(r0, right), send(r0, left)
    v = jnp.concatenate([v, send(v, move(dx=1))], axis=0)
    l2, u2 = send(l1, right), send(u1, left)

    scal = jnp.stack([logit_stretch, logit_offset])
    idx = jnp.concatenate(
        [
            lax.dynamic_slice_in_dim(index, at(y, x + a, c + o) * rows, rows)
            for a in (0, 1)
            for o in (0, 1)
        ]
    )[None]

    def work(steps, rs, carry=()):
        to = jnp.stack([(y + k) % NY for k in steps]).astype(jnp.int32)
        base = (to * (NX * NC) + x * NC + c) * rows
        return pairs(base.astype(jnp.int32), to, scal, idx, v, rs, carry)

    carry = work((0, -1, 1), (r0, l1, u1))
    l2, u2, *carry = tie(l2, u2, *carry)
    l3, u3 = send(l2, right), send(u2, left)
    carry = work((-2, 2), (l2, u2), carry)
    l3, u3, *carry = tie(l3, u3, *carry)
    r4 = send(jnp.where(c == 0, l3, u3), split(1))
    carry = work((-3, 3), (l3, u3), carry)
    ds, sums, do = work((4,), (r4,), carry)

    do = lax.psum_scatter(do, "y", scatter_dimension=0, tiled=True)
    dx = send(ds[2 * rows :], move(dx=1))
    sums = lax.psum(sums, "c")
    sums = lax.psum(sums, "z")
    sums, dx = tie(sums, dx)
    ds = ds[: 2 * rows] + dx
    dc = send(ds[rows:], move(dc=1))
    sums = lax.psum(sums, ("x", "h"))
    sums = lax.psum(sums, "y")
    ds = ds[:rows] + dc
    count = 1.0 * lax.axis_size(REP) * batch * batch
    s = jnp.sum(sums, axis=1) / count
    return ds[None], do[None], s[0], s[1], s[2]


def solution(mesh):
    axes = Mesh(mesh.devices.reshape(NY, NX, NC, NZ, NH), BLK + REP)
    split_of = P(REP, BLK, None)
    in_specs = (split_of, split_of, P(REP, None), P(), P())
    out_specs = (split_of, split_of, P(), P(), P())
    return jax.shard_map(local, mesh=axes, in_specs=in_specs, out_specs=out_specs, check_vma=False)
```

```python
import functools
import math

import jax
import jax.numpy as jnp
from jax import lax
from jax.experimental import pallas as pl
from jax.experimental.pallas import tpu as pltpu
from jax.sharding import Mesh
from jax.sharding import PartitionSpec as P

NY, NX, NC, NZ, NH = 8, 2, 2, 8, 2
BLK, REP = ("y", "x", "c"), ("z", "h")


def at(y, x, c):
    return (y % NY) * NX * NC + (x % NX) * NC + (c % NC)


def move(dy=0, dx=0, dc=0):
    return [
        (at(y, x, c), at(y + dy, x + dx, c + dc))
        for y in range(NY)
        for x in range(NX)
        for c in range(NC)
    ]


def split(step):
    return [
        (at(y, x, c), at(y + (step if c == 0 else -step), x, c))
        for y in range(NY)
        for x in range(NX)
        for c in range(NC)
    ]


def pair_kernel(unit, first, groups, base_ref, to_ref, scal_ref, idx_ref, *rest):
    n = sum(groups)
    v_hbm, r_hbm, rest = rest[:2], rest[2 : 2 + n], rest[2 + n :]
    if not first:
        ds_in, sums_in, _, *rest = rest
    ds_ref, sums_ref, do_ref, v_ref, held, out_sems = rest
    half = v_hbm[0].shape[0]
    width = r_hbm[0].shape[0]
    m = 2 * half
    stretch = scal_ref[0]
    offset = scal_ref[1]
    scale = stretch * unit
    matched = idx_ref[...]
    sums = [jnp.zeros((8, m), jnp.float32) for _ in range(3)]
    for i in range(2):
        v_ref[i * half : (i + 1) * half, :] = v_hbm[i][...]
    v = v_ref[...]
    stores = {}
    k = 0
    for g, size in enumerate(groups):
        slot = g % 2
        for store in stores.pop(slot, []):
            store.wait()
        r = jnp.concatenate([r_hbm[k + i][...] for i in range(size)], axis=0)
        y = (
            lax.dot_general(r, v, (((1,), (1,)), ((), ())), preferred_element_type=jnp.float32)
            * unit
        )
        x = stretch * y + offset
        lane = lax.broadcasted_iota(jnp.int32, (width, m), 0)
        hit = jnp.concatenate([base_ref[k + i] + lane == matched for i in range(size)], axis=0)
        t = jnp.where(hit, -x, x)
        e = jnp.exp(-jnp.abs(t))
        inv = 1.0 / (1.0 + e)
        sig = jnp.where(t >= 0, inv, e * inv)
        grad = jnp.where(hit, -sig, sig)
        for i, a in enumerate((jnp.maximum(t, 0.0) + jnp.log1p(e), grad * y, grad)):
            sums[i] += jnp.sum(a.reshape(size * width // 8, 8, m), axis=0)
        coef = (grad * scale).astype(jnp.bfloat16)
        held[slot, : size * width, :] = jnp.dot(coef, v, preferred_element_type=jnp.float32)
        stores[slot] = []
        for i in range(size):
            rows = pl.ds(pl.multiple_of(to_ref[k + i] * width, width), width)
            stores[slot].append(
                pltpu.make_async_copy(
                    held.at[slot, pl.ds(i * width, width)], do_ref.at[rows], out_sems.at[slot, i]
                )
            )
            stores[slot][i].start()
        part = lax.dot_general(
            coef, r, (((0,), (0,)), ((), ())), preferred_element_type=jnp.float32
        )
        if g:
            ds_ref[...] += part
        elif first:
            ds_ref[...] = part
        else:
            ds_ref[...] = ds_in[...] + part
        k += size
    for i, a in enumerate(sums):
        s = a[:, :128]
        for j in range(128, m, 128):
            s += a[:, j : j + 128]
        s = jnp.sum(s, axis=0, keepdims=True)
        sums_ref[i : i + 1, :] = s if first else s + sums_in[i : i + 1, :]
    for slot in sorted(stores):
        for store in stores[slot]:
            store.wait()


def pairs(base, to, scal, idx, vs, rs, groups, carry=()):
    half, d = vs[0].shape
    m = 2 * half
    width = rs[0].shape[0]
    n = len(rs)
    cols = n * width
    vm = pl.BlockSpec(memory_space=pltpu.VMEM)
    sm = pl.BlockSpec(memory_space=pltpu.SMEM)
    hbm = pl.BlockSpec(memory_space=pltpu.HBM)
    args = [base, to, scal, idx, *vs, *rs, *carry]
    first = len(args) - 3
    return pl.pallas_call(
        functools.partial(pair_kernel, 1.0 / math.sqrt(d), not carry, groups),
        out_shape=[
            jax.ShapeDtypeStruct((m, d), jnp.float32),
            jax.ShapeDtypeStruct((3, 128), jnp.float32),
            jax.ShapeDtypeStruct((NY * width, d), jnp.float32),
        ],
        in_specs=[sm, sm, sm, vm] + [vm] * (2 + n) + ([vm, vm, hbm] if carry else []),
        out_specs=[vm, vm, hbm],
        scratch_shapes=[
            pltpu.VMEM((m, d), jnp.bfloat16),
            pltpu.VMEM((2, max(groups) * width, d), jnp.float32),
            pltpu.SemaphoreType.DMA((2, max(groups))),
        ],
        input_output_aliases={first + i: i for i in range(3)} if carry else {},
        compiler_params=pltpu.CompilerParams(vmem_limit_bytes=48 * 1024 * 1024),
        cost_estimate=pl.CostEstimate(
            flops=6 * m * cols * d,
            bytes_accessed=2 * (m + cols) * d + 4 * (2 * m + cols) * d,
            transcendentals=3 * m * cols,
        ),
    )(*args)


def local(visit_embeds, result_embeds, matched_result_index, logit_stretch, logit_offset):
    v0 = visit_embeds[0]
    r0 = result_embeds[0]
    rows = v0.shape[0]
    index = matched_result_index[0]
    batch = index.shape[0]
    me = lax.axis_index(BLK)
    y, x, c = me // (NX * NC), (me // NC) % NX, me % NC
    tie = lambda *xs: lax.optimization_barrier(xs)
    send = lambda a, p: lax.ppermute(a, BLK, p)
    with_a, with_b = split(1), split(-1)
    side = 2 * c - 1

    a1, b1 = send(r0, with_a), send(r0, with_b)
    own = jnp.concatenate([v0, send(v0, move(dc=1))], axis=0)
    vs = (own, send(own, move(dx=1)))
    a2, b2 = send(a1, with_a), send(b1, with_b)
    a3, b3 = send(a2, with_a), send(b2, with_b)

    scal = jnp.stack([logit_stretch, logit_offset])
    idx = jnp.concatenate(
        [
            lax.dynamic_slice_in_dim(index, at(y, x + a, c + o) * rows, rows)
            for a in (0, 1)
            for o in (0, 1)
        ]
    )[None]

    def work(steps, rs, groups, carry=()):
        to = jnp.stack([(y + side * k) % NY for k in steps]).astype(jnp.int32)
        base = (to * (NX * NC) + x * NC + c) * rows
        return pairs(base.astype(jnp.int32), to, scal, idx, vs, rs, groups, carry)

    carry = work((0, 1, -1, 2, -2), (r0, a1, b1, a2, b2), (1, 2, 2))
    a3, b3, *carry = tie(a3, b3, *carry)
    a4 = send(a3, with_a)
    carry = work((3, -3), (a3, b3), (2,), carry)
    ds, sums, do = work((4,), (a4,), (1,), carry)

    do = lax.psum_scatter(do, "y", scatter_dimension=0, tiled=True)
    dx = send(ds[2 * rows :], move(dx=1))
    sums = lax.psum(sums, "c")
    sums = lax.psum(sums, "z")
    sums = lax.psum(sums, ("x", "h"))
    sums, dx = tie(sums, dx)
    ds = ds[: 2 * rows] + dx
    dc = send(ds[rows:], move(dc=1))
    sums = lax.psum(sums, "y")
    ds = ds[:rows] + dc
    count = 1.0 * lax.axis_size(REP) * batch * batch
    s = jnp.sum(sums, axis=1) / count
    return ds[None], do[None], s[0], s[1], s[2]


def solution(mesh):
    axes = Mesh(mesh.devices.reshape(NY, NX, NC, NZ, NH), BLK + REP)
    split_of = P(REP, BLK, None)
    in_specs = (split_of, split_of, P(REP, None), P(), P())
    out_specs = (split_of, split_of, P(), P(), P())
    return jax.shard_map(local, mesh=axes, in_specs=in_specs, out_specs=out_specs, check_vma=False)
```

```python
import functools
import math

import jax
import jax.numpy as jnp
from jax import lax
from jax.experimental import pallas as pl
from jax.experimental.pallas import tpu as pltpu
from jax.sharding import Mesh
from jax.sharding import PartitionSpec as P

NY, NX, NC, NZ, NH = 8, 2, 2, 8, 2
BLK, REP = ("y", "x", "c"), ("z", "h")


def at(y, x, c):
    return (y % NY) * NX * NC + (x % NX) * NC + (c % NC)


def move(dy=0, dx=0, dc=0):
    return [
        (at(y, x, c), at(y + dy, x + dx, c + dc))
        for y in range(NY)
        for x in range(NX)
        for c in range(NC)
    ]


def split(step):
    return [
        (at(y, x, c), at(y + (step if c == 0 else -step), x, c))
        for y in range(NY)
        for x in range(NX)
        for c in range(NC)
    ]


def pair_kernel(unit, first, groups, base_ref, to_ref, scal_ref, idx_ref, *rest):
    n = sum(groups)
    v_hbm, r_hbm, rest = rest[:2], rest[2 : 2 + n], rest[2 + n :]
    if not first:
        ds_in, sums_in, _, *rest = rest
    ds_ref, sums_ref, do_ref, v_ref, held, out_sems = rest
    half = v_hbm[0].shape[0]
    width = r_hbm[0].shape[0]
    m = 2 * half
    stretch = scal_ref[0]
    offset = scal_ref[1]
    scale = stretch * unit
    matched = idx_ref[...]
    sums = [jnp.zeros((8, m), jnp.float32) for _ in range(3)]
    for i in range(2):
        v_ref[i * half : (i + 1) * half, :] = v_hbm[i][...]
    v = v_ref[...]
    stores = {}
    k = 0
    for g, size in enumerate(groups):
        slot = g % 2
        for store in stores.pop(slot, []):
            store.wait()
        r = jnp.concatenate([r_hbm[k + i][...] for i in range(size)], axis=0)
        y = (
            lax.dot_general(r, v, (((1,), (1,)), ((), ())), preferred_element_type=jnp.float32)
            * unit
        )
        x = stretch * y + offset
        lane = lax.broadcasted_iota(jnp.int32, (width, m), 0)
        hit = jnp.concatenate([base_ref[k + i] + lane == matched for i in range(size)], axis=0)
        t = jnp.where(hit, -x, x)
        e = jnp.exp(-jnp.abs(t))
        inv = 1.0 / (1.0 + e)
        sig = jnp.where(t >= 0, inv, e * inv)
        grad = jnp.where(hit, -sig, sig)
        for i, a in enumerate((jnp.maximum(t, 0.0) + jnp.log1p(e), grad * y, grad)):
            sums[i] += jnp.sum(a.reshape(size * width // 8, 8, m), axis=0)
        coef = (grad * scale).astype(jnp.bfloat16)
        held[slot, : size * width, :] = jnp.dot(coef, v, preferred_element_type=jnp.float32)
        stores[slot] = []
        for i in range(size):
            rows = pl.ds(pl.multiple_of(to_ref[k + i] * width, width), width)
            stores[slot].append(
                pltpu.make_async_copy(
                    held.at[slot, pl.ds(i * width, width)], do_ref.at[rows], out_sems.at[slot, i]
                )
            )
            stores[slot][i].start()
        part = lax.dot_general(
            coef, r, (((0,), (0,)), ((), ())), preferred_element_type=jnp.float32
        )
        if g:
            ds_ref[...] += part
        elif first:
            ds_ref[...] = part
        else:
            ds_ref[...] = ds_in[...] + part
        k += size
    for i, a in enumerate(sums):
        s = a[:, :128]
        for j in range(128, m, 128):
            s += a[:, j : j + 128]
        s = jnp.sum(s, axis=0, keepdims=True)
        sums_ref[i : i + 1, :] = s if first else s + sums_in[i : i + 1, :]
    for slot in sorted(stores):
        for store in stores[slot]:
            store.wait()


def pairs(base, to, scal, idx, vs, rs, groups, carry=()):
    half, d = vs[0].shape
    m = 2 * half
    width = rs[0].shape[0]
    n = len(rs)
    cols = n * width
    vm = pl.BlockSpec(memory_space=pltpu.VMEM)
    sm = pl.BlockSpec(memory_space=pltpu.SMEM)
    hbm = pl.BlockSpec(memory_space=pltpu.HBM)
    args = [base, to, scal, idx, *vs, *rs, *carry]
    first = len(args) - 3
    return pl.pallas_call(
        functools.partial(pair_kernel, 1.0 / math.sqrt(d), not carry, groups),
        out_shape=[
            jax.ShapeDtypeStruct((m, d), jnp.float32),
            jax.ShapeDtypeStruct((3, 128), jnp.float32),
            jax.ShapeDtypeStruct((NY * width, d), jnp.float32),
        ],
        in_specs=[sm, sm, sm, vm] + [vm] * (2 + n) + ([vm, vm, hbm] if carry else []),
        out_specs=[vm, vm, hbm],
        scratch_shapes=[
            pltpu.VMEM((m, d), jnp.bfloat16),
            pltpu.VMEM((2, max(groups) * width, d), jnp.float32),
            pltpu.SemaphoreType.DMA((2, max(groups))),
        ],
        input_output_aliases={first + i: i for i in range(3)} if carry else {},
        compiler_params=pltpu.CompilerParams(vmem_limit_bytes=48 * 1024 * 1024),
        cost_estimate=pl.CostEstimate(
            flops=6 * m * cols * d,
            bytes_accessed=2 * (m + cols) * d + 4 * (2 * m + cols) * d,
            transcendentals=3 * m * cols,
        ),
    )(*args)


def local(visit_embeds, result_embeds, matched_result_index, logit_stretch, logit_offset):
    v0 = visit_embeds[0]
    r0 = result_embeds[0]
    rows = v0.shape[0]
    index = matched_result_index[0]
    batch = index.shape[0]
    me = lax.axis_index(BLK)
    y, x, c = me // (NX * NC), (me // NC) % NX, me % NC
    tie = lambda *xs: lax.optimization_barrier(xs)
    send = lambda a, p: lax.ppermute(a, BLK, p)
    with_a, with_b = split(1), split(-1)
    side = 2 * c - 1

    a1, b1 = send(r0, with_a), send(r0, with_b)
    own = jnp.concatenate([v0, send(v0, move(dc=1))], axis=0)
    vs = (own, send(own, move(dx=1)))
    a2, b2 = send(a1, with_a), send(b1, with_b)
    a3, b3 = send(a2, with_a), send(b2, with_b)

    scal = jnp.stack([logit_stretch, logit_offset])
    idx = jnp.concatenate(
        [
            lax.dynamic_slice_in_dim(index, at(y, x + a, c + o) * rows, rows)
            for a in (0, 1)
            for o in (0, 1)
        ]
    )[None]

    def work(steps, rs, groups, carry=()):
        to = jnp.stack([(y + side * k) % NY for k in steps]).astype(jnp.int32)
        base = (to * (NX * NC) + x * NC + c) * rows
        return pairs(base.astype(jnp.int32), to, scal, idx, vs, rs, groups, carry)

    carry = work((1, -1, 2, -2), (a1, b1, a2, b2), (2, 2))
    a3, b3, *carry = tie(a3, b3, *carry)
    a4 = send(a3, with_a)
    carry = work((0, 3, -3), (r0, a3, b3), (1, 2), carry)
    ds, sums, do = work((4,), (a4,), (1,), carry)

    do = lax.psum_scatter(do, "y", scatter_dimension=0, tiled=True)
    dx = send(ds[2 * rows :], move(dx=1))
    sums = lax.psum(sums, "c")
    sums = lax.psum(sums, "z")
    sums = lax.psum(sums, ("x", "h"))
    sums, dx = tie(sums, dx)
    ds = ds[: 2 * rows] + dx
    dc = send(ds[rows:], move(dc=1))
    sums = lax.psum(sums, "y")
    ds = ds[:rows] + dc
    count = 1.0 * lax.axis_size(REP) * batch * batch
    s = jnp.sum(sums, axis=1) / count
    return ds[None], do[None], s[0], s[1], s[2]


def solution(mesh):
    axes = Mesh(mesh.devices.reshape(NY, NX, NC, NZ, NH), BLK + REP)
    split_of = P(REP, BLK, None)
    in_specs = (split_of, split_of, P(REP, None), P(), P())
    out_specs = (split_of, split_of, P(), P(), P())
    return jax.shard_map(local, mesh=axes, in_specs=in_specs, out_specs=out_specs, check_vma=False)
```

```python
import functools
import math

import jax
import jax.numpy as jnp
from jax import lax
from jax.experimental import pallas as pl
from jax.experimental.pallas import tpu as pltpu
from jax.sharding import Mesh
from jax.sharding import PartitionSpec as P

NY, NX, NC, NZ, NH = 8, 2, 2, 8, 2
BLK, REP = ("y", "x", "c"), ("z", "h")


def at(y, x, c):
    return (y % NY) * NX * NC + (x % NX) * NC + (c % NC)


def move(dy=0, dx=0, dc=0):
    return [
        (at(y, x, c), at(y + dy, x + dx, c + dc))
        for y in range(NY)
        for x in range(NX)
        for c in range(NC)
    ]


def split(step):
    return [
        (at(y, x, c), at(y + (step if c == 0 else -step), x, c))
        for y in range(NY)
        for x in range(NX)
        for c in range(NC)
    ]


def pair_kernel(unit, first, groups, base_ref, to_ref, scal_ref, idx_ref, *rest):
    n = sum(groups)
    v_hbm, r_hbm, rest = rest[:2], rest[2 : 2 + n], rest[2 + n :]
    if not first:
        ds_in, sums_in, _, *rest = rest
    ds_ref, sums_ref, do_ref, v_ref, held, out_sems = rest
    half = v_hbm[0].shape[0]
    width = r_hbm[0].shape[0]
    m = 2 * half
    stretch = scal_ref[0]
    offset = scal_ref[1]
    scale = stretch * unit
    matched = idx_ref[...]
    sums = [jnp.zeros((8, m), jnp.float32) for _ in range(3)]
    for i in range(2):
        v_ref[i * half : (i + 1) * half, :] = v_hbm[i][...]
    v = v_ref[...]
    stores = {}
    k = 0
    for g, size in enumerate(groups):
        slot = g % 2
        for store in stores.pop(slot, []):
            store.wait()
        r = jnp.concatenate([r_hbm[k + i][...] for i in range(size)], axis=0)
        y = (
            lax.dot_general(r, v, (((1,), (1,)), ((), ())), preferred_element_type=jnp.float32)
            * unit
        )
        x = stretch * y + offset
        lane = lax.broadcasted_iota(jnp.int32, (width, m), 0)
        hit = jnp.concatenate([base_ref[k + i] + lane == matched for i in range(size)], axis=0)
        t = jnp.where(hit, -x, x)
        e = jnp.exp(-jnp.abs(t))
        inv = 1.0 / (1.0 + e)
        sig = jnp.where(t >= 0, inv, e * inv)
        grad = jnp.where(hit, -sig, sig)
        for i, a in enumerate((jnp.maximum(t, 0.0) + jnp.log1p(e), grad * y, grad)):
            sums[i] += jnp.sum(a.reshape(size * width // 8, 8, m), axis=0)
        coef = (grad * scale).astype(jnp.bfloat16)
        held[slot, : size * width, :] = jnp.dot(coef, v, preferred_element_type=jnp.float32)
        stores[slot] = []
        for i in range(size):
            rows = pl.ds(pl.multiple_of(to_ref[k + i] * width, width), width)
            stores[slot].append(
                pltpu.make_async_copy(
                    held.at[slot, pl.ds(i * width, width)], do_ref.at[rows], out_sems.at[slot, i]
                )
            )
            stores[slot][i].start()
        part = lax.dot_general(
            coef, r, (((0,), (0,)), ((), ())), preferred_element_type=jnp.float32
        )
        if g:
            ds_ref[...] += part
        elif first:
            ds_ref[...] = part
        else:
            ds_ref[...] = ds_in[...] + part
        k += size
    for i, a in enumerate(sums):
        s = a[:, :128]
        for j in range(128, m, 128):
            s += a[:, j : j + 128]
        s = jnp.sum(s, axis=0, keepdims=True)
        sums_ref[i : i + 1, :] = s if first else s + sums_in[i : i + 1, :]
    for slot in sorted(stores):
        for store in stores[slot]:
            store.wait()


def pairs(base, to, scal, idx, vs, rs, groups, carry=()):
    half, d = vs[0].shape
    m = 2 * half
    width = rs[0].shape[0]
    n = len(rs)
    cols = n * width
    vm = pl.BlockSpec(memory_space=pltpu.VMEM)
    sm = pl.BlockSpec(memory_space=pltpu.SMEM)
    hbm = pl.BlockSpec(memory_space=pltpu.HBM)
    args = [base, to, scal, idx, *vs, *rs, *carry]
    first = len(args) - 3
    return pl.pallas_call(
        functools.partial(pair_kernel, 1.0 / math.sqrt(d), not carry, groups),
        out_shape=[
            jax.ShapeDtypeStruct((m, d), jnp.float32),
            jax.ShapeDtypeStruct((3, 128), jnp.float32),
            jax.ShapeDtypeStruct((NY * width, d), jnp.float32),
        ],
        in_specs=[sm, sm, sm, vm] + [vm] * (2 + n) + ([vm, vm, hbm] if carry else []),
        out_specs=[vm, vm, hbm],
        scratch_shapes=[
            pltpu.VMEM((m, d), jnp.bfloat16),
            pltpu.VMEM((2, max(groups) * width, d), jnp.float32),
            pltpu.SemaphoreType.DMA((2, max(groups))),
        ],
        input_output_aliases={first + i: i for i in range(3)} if carry else {},
        compiler_params=pltpu.CompilerParams(vmem_limit_bytes=48 * 1024 * 1024),
        cost_estimate=pl.CostEstimate(
            flops=6 * m * cols * d,
            bytes_accessed=2 * (m + cols) * d + 4 * (2 * m + cols) * d,
            transcendentals=3 * m * cols,
        ),
    )(*args)


def local(visit_embeds, result_embeds, matched_result_index, logit_stretch, logit_offset):
    v0 = visit_embeds[0]
    r0 = result_embeds[0]
    rows = v0.shape[0]
    index = matched_result_index[0]
    batch = index.shape[0]
    me = lax.axis_index(BLK)
    y, x, c = me // (NX * NC), (me // NC) % NX, me % NC
    tie = lambda *xs: lax.optimization_barrier(xs)
    send = lambda a, p: lax.ppermute(a, BLK, p)
    with_a, with_b = split(1), split(-1)
    side = 2 * c - 1

    a1, b1 = send(r0, with_a), send(r0, with_b)
    own = jnp.concatenate([v0, send(v0, move(dc=1))], axis=0)
    vs = (own, send(own, move(dx=1)))
    a2, b2 = send(a1, with_a), send(b1, with_b)
    a3, b3 = send(a2, with_a), send(b2, with_b)

    scal = jnp.stack([logit_stretch, logit_offset])
    idx = jnp.concatenate(
        [
            lax.dynamic_slice_in_dim(index, at(y, x + a, c + o) * rows, rows)
            for a in (0, 1)
            for o in (0, 1)
        ]
    )[None]

    def work(steps, rs, groups, carry=()):
        to = jnp.stack([(y + side * k) % NY for k in steps]).astype(jnp.int32)
        base = (to * (NX * NC) + x * NC + c) * rows
        return pairs(base.astype(jnp.int32), to, scal, idx, vs, rs, groups, carry)

    carry = work((1, -1, 2, -2), (a1, b1, a2, b2), (2, 2))
    a4 = send(b3, with_b)
    carry = work((0, 3, -3), (r0, a3, b3), (1, 2), carry)
    ds, sums, do = work((4,), (a4,), (1,), carry)

    do = lax.psum_scatter(do, "y", scatter_dimension=0, tiled=True)
    dx = send(ds[2 * rows :], move(dx=1))
    sums = lax.psum(sums, "c")
    sums = lax.psum(sums, "z")
    sums = lax.psum(sums, ("x", "h"))
    sums, dx = tie(sums, dx)
    ds = ds[: 2 * rows] + dx
    dc = send(ds[rows:], move(dc=1))
    sums = lax.psum(sums, "y")
    ds = ds[:rows] + dc
    count = 1.0 * lax.axis_size(REP) * batch * batch
    s = jnp.sum(sums, axis=1) / count
    return ds[None], do[None], s[0], s[1], s[2]


def solution(mesh):
    axes = Mesh(mesh.devices.reshape(NY, NX, NC, NZ, NH), BLK + REP)
    split_of = P(REP, BLK, None)
    in_specs = (split_of, split_of, P(REP, None), P(), P())
    out_specs = (split_of, split_of, P(), P(), P())
    return jax.shard_map(local, mesh=axes, in_specs=in_specs, out_specs=out_specs, check_vma=False)
```
